32 devices in a mesh: rows: 16 (over z, y, core), rank: 2 (over x).
Axes of the slice: x: 2, y: 2, z: 4, core: 2. Of those that a mesh axis runs over, the one named last changes fastest.
Arguments:
- factor: bfloat16 [16384, 16384], P('rows', 'rank'), may hold values from -0.046875 to 0.046875
- probes: bfloat16 [16384, 256], P('rows'), may hold values from -1.5 to 1.5
- cotangent: bfloat16 [16384, 256], P('rows'), may hold values from -1.5 to 1.5
- core_inverse: bfloat16 [16384, 2, 8192], P('rank', None, 'rows'), may hold values from -0.046875 to 0.046875
- pivots: int32 [16384], replicated, may hold values from 0 to 16383, as said below
- noise: float32 [1], replicated, may hold values from 0.5 to 2
Outputs:
- probe_grad: bfloat16 [16384, 256], P('rows')
- factor_grad: bfloat16 [16384, 16384], P('rows', 'rank')
The draws below stay inside these ranges and needn't reach their ends.
Inputs may be any that keep to these rules, and one draw needn't show every extreme that they name: `pivots`: distinct slab rows; rows 0 and 16383 are always among them.
All inputs are finite; a program needn't handle non-finite values.
Results may differ from the reference program's by a relative error of at most 0.001.
Values sent between devices are 32-bit elements; how exact they have to be, the bound alone decides.
A program may use at most 128 MiB of HBM per device.

```python
import math
import jax
import jax.numpy as jnp
from jax import lax

K = 16384
B = 256
NS = 16384
KB = 8192
N_RANK = 2


def draw_pivots(key, part):
    first = jax.random.fold_in(key, 11)
    second = jax.random.fold_in(key, 23)
    scores = jax.random.permutation(first, NS).astype(jnp.int32)
    scores = scores.at[0].set(-2).at[NS - 1].set(-1)
    order = jnp.argsort(scores, stable=True).astype(jnp.int32)
    chosen = order[:K]
    return jax.random.permutation(second, chosen).astype(jnp.int32)


def level_of(rng, dims, pieces, smallest, top_value):
    def one(axis_at, blocks):
        steps = jax.random.uniform(jax.random.fold_in(jax.random.fold_in(rng, 6), axis_at), (blocks,), jnp.float32, smallest / len(pieces), top_value / len(pieces))
        return jnp.repeat(jnp.exp(steps), dims[axis_at] // blocks).reshape((-1,) + (1,) * (len(dims) - axis_at - 1))

    loudness = one(*pieces[0])
    for cut in pieces[1:]:
        loudness = loudness * one(*cut)
    return loudness


def gaussian(key, shape, spread, bound, pieces=(), held_as=jnp.bfloat16):
    level = level_of(key, shape, pieces, -0.22, 0.18) if pieces else 1.0
    result = jax.random.normal(key, shape, jnp.float32) * spread * level
    return jnp.minimum(jnp.maximum(result, -bound), bound).astype(held_as)


def setup_inputs(seed: int = 0) -> dict:
    streams_of = jax.random.split(jax.random.key(seed), 7)
    factor = gaussian(streams_of[0], (NS, K), NS ** -0.5, 0.046875, ((0, 16), (1, 2)))
    probes = gaussian(streams_of[1], (NS, B), 0.25, 1.5, ((0, 16),))
    cotangent = gaussian(streams_of[2], (NS, B), 0.25, 1.5, ((0, 16),))
    core_inverse = gaussian(streams_of[3], (K, N_RANK, KB), K ** -0.5, 0.046875, ((0, 2), (2, 16)))
    pivots = draw_pivots(jax.random.fold_in(streams_of[6], 71), 0)
    noise = jnp.clip(jnp.exp(jax.random.uniform(streams_of[5], (1,), jnp.float32, math.log(0.5), math.log(2.0))), 0.5, 2.0)
    return dict(factor=factor, probes=probes, cotangent=cotangent, core_inverse=core_inverse, pivots=pivots, noise=noise)


def reference(factor, probes, cotangent, core_inverse, pivots, noise):
    scale = noise[0]
    highest = lax.Precision.HIGHEST
    contract = (((0,), (0,)), ((), ()))
    coefs = lax.dot_general(factor, probes, contract, preferred_element_type=jnp.float32)
    duals_in = lax.dot_general(factor, cotangent, contract, preferred_element_type=jnp.float32)
    kblock = min(K, 1024)
    core_blocks = core_inverse.reshape(K // kblock, kblock, K)

    def weight_block(core_blk):
        return jnp.dot(core_blk.astype(jnp.float32), coefs, precision=highest, preferred_element_type=jnp.float32)

    weights = lax.map(weight_block, core_blocks).reshape(K, B)

    def dual_step(carry, items):
        core_blk, dual_blk = items
        term = lax.dot_general(core_blk.astype(jnp.float32), dual_blk, contract, precision=highest, preferred_element_type=jnp.float32)
        return carry + term, None

    duals, unused = lax.scan(dual_step, jnp.zeros((K, B), jnp.float32), (core_blocks, duals_in.reshape(K // kblock, kblock, B)))
    pivot_rank = jnp.full((NS,), K, jnp.int32).at[pivots].set(jnp.arange(K, dtype=jnp.int32))
    block = min(NS, 1024)
    columns = jnp.arange(K, dtype=jnp.int32)

    def one_block(items):
        fac_blk, cot_blk, probe_blk, rank_blk = items
        correction = jnp.dot(fac_blk.astype(jnp.float32), duals, precision=highest, preferred_element_type=jnp.float32)
        pgrad = ((cot_blk.astype(jnp.float32) - correction) / scale).astype(jnp.bfloat16)
        first = lax.dot_general(cot_blk.astype(jnp.float32), weights, (((1,), (1,)), ((), ())), precision=highest, preferred_element_type=jnp.float32)
        second = lax.dot_general(probe_blk.astype(jnp.float32), duals, (((1,), (1,)), ((), ())), precision=highest, preferred_element_type=jnp.float32)
        grads = -(first + second) / scale
        grads = jnp.where(columns[None, :] > rank_blk[:, None], jnp.float32(0.0), grads)
        return pgrad, grads.astype(jnp.bfloat16)

    probe_grad, factor_grad = lax.map(one_block, (factor.reshape(NS // block, block, K), cotangent.reshape(NS // block, block, B), probes.reshape(NS // block, block, B), pivot_rank.reshape(NS // block, block)))
    return probe_grad.reshape(NS, B), factor_grad.reshape(NS, K)
```

```python
import functools

import jax
import jax.numpy as jnp
from jax import lax
from jax.experimental import pallas as pl
from jax.experimental.pallas import tpu as pltpu
from jax.sharding import PartitionSpec as P

MESH = pl.DeviceIdType.MESH
VMEM = pl.BlockSpec(memory_space=pltpu.VMEM)
ANY = pl.BlockSpec(memory_space=pl.ANY)
F32 = jnp.float32
BF16 = jnp.bfloat16
SUBS = 2
NT = (((1,), (1,)), ((), ()))


def halves(x):
    high = x.astype(BF16)
    low = (x - high.astype(F32)).astype(BF16)
    return jnp.concatenate([high, low], axis=0)


class Ring:
    def __init__(self, n_rows):
        self.n = n_rows // 2
        row = lax.axis_index("rows")
        self.row = row
        self.rank = lax.axis_index("rank")
        self.core = row % 2
        chip = row // 2
        odd = chip % 2
        self.pos = (1 - odd) * (chip // 2) + odd * (self.n - 1 - chip // 2)
        self.next = [self.device(self.pos + 1), self.device(self.pos - 1)]
        self.sibling = (self.owner(self.pos, True), self.rank)
        self.partner = (row, 1 - self.rank)

    def owner(self, pos, other=False):
        pos = (pos + 2 * self.n) % self.n
        upper = (2 * pos) // self.n
        chip = (1 - upper) * (2 * pos) + upper * (2 * (self.n - 1 - pos) + 1)
        core = (1 - self.core) if other else self.core
        return 2 * chip + core

    def device(self, pos):
        return (self.owner(pos), self.rank)

    def enter(self, with_partner):
        barrier = pltpu.get_barrier_semaphore()
        peers = self.next + [self.sibling] + ([self.partner] if with_partner else [])
        for peer in peers:
            pl.semaphore_signal(barrier, inc=1, device_id=peer, device_id_type=MESH)
        pl.semaphore_wait(barrier, len(peers))


def remote(src, dst, send, recv, device):
    return pltpu.make_async_remote_copy(
        src_ref=src, dst_ref=dst, send_sem=send, recv_sem=recv, device_id=device, device_id_type=MESH
    )


class Gather:
    def __init__(self, ring, buf, ring_sems, sib_sems):
        self.ring, self.buf = ring, buf
        self.rs, self.ss = ring_sems, sib_sems
        self.half = buf.shape[1] // 2
        self.sub = self.half // SUBS

    def at(self, d, t):
        return self.ring.pos - t if d == 0 else self.ring.pos + t

    def part(self, owner, d, u):
        return self.buf.at[owner, pl.ds(d * self.half + u * self.sub, self.sub)]

    def hop(self, d, u, t):
        ref = self.part(self.ring.owner(self.at(d, t)), d, u)
        return remote(ref, ref, self.rs.at[0, d, u, t], self.rs.at[1, d, u, t], self.ring.next[d])

    def hop_in(self, d, u, t):
        ref = self.part(self.ring.owner(self.at(d, t + 1)), d, u)
        return remote(ref, ref, self.rs.at[0, d, u, t], self.rs.at[1, d, u, t], self.ring.next[d])

    def across(self, d, u, t):
        ref = self.part(self.ring.owner(self.at(d, t)), d, u)
        return remote(ref, ref, self.ss.at[0, d, u, t], self.ss.at[1, d, u, t], self.ring.sibling)

    def across_in(self, d, u, t):
        ref = self.part(self.ring.owner(self.at(d, t), True), d, u)
        return remote(ref, ref, self.ss.at[0, d, u, t], self.ss.at[1, d, u, t], self.ring.sibling)

    def step(self, t, first=False, last=False):
        for u in range(SUBS):
            for d in range(2):
                if not first:
                    self.hop_in(d, u, t - 1).wait_recv()
                if not last:
                    self.hop(d, u, t).start()
                self.across(d, u, t).start()

    def wait_across(self, t):
        for u in range(SUBS):
            for d in range(2):
                self.across_in(d, u, t).wait_recv()

    def mine(self, d, t):
        return self.ring.owner(self.at(d, t))

    def theirs(self, d, t):
        return self.ring.owner(self.at(d, t), True)

    def finish(self):
        @pl.loop(0, self.ring.n)
        def _(t):
            for u in range(SUBS):
                for d in range(2):
                    self.across(d, u, t).wait_send()

        @pl.loop(0, self.ring.n - 1)
        def _(t):
            for u in range(SUBS):
                for d in range(2):
                    self.hop(d, u, t).wait_send()


class Scatter:
    def __init__(self, ring, term, land, sib_in, sib_out, ring_sems, sib_sems):
        self.ring, self.term = ring, term
        self.land, self.sib_in, self.sib_out = land, sib_in, sib_out
        self.rs, self.ss = ring_sems, sib_sems
        self.sub = land.shape[2] // SUBS

    def at(self, d, t):
        return self.ring.pos - 1 - t if d == 0 else self.ring.pos + 1 + t

    def across(self, d, t):
        return remote(
            self.sib_out.at[t, d], self.sib_in.at[t, d], self.ss.at[0, d, t], self.ss.at[1, d, t], self.ring.sibling
        )

    def rows(self, u):
        return pl.ds(u * self.sub, self.sub)

    def hop(self, d, u, t, first=False):
        src = self.sib_in.at[0, d, self.rows(u)] if first else self.land.at[t - 1, d, self.rows(u)]
        dst = self.land.at[t, d, self.rows(u)]
        return remote(src, dst, self.rs.at[0, d, u, t], self.rs.at[1, d, u, t], self.ring.next[d])

    def prepare(self, t):
        for d in range(2):
            self.sib_out[t, d] = self.term(self.ring.owner(self.at(d, t), True), d)
            self.across(d, t).start()
        own = [self.term(self.ring.owner(self.at(d, t)), d) for d in range(2)]
        for d in range(2):
            self.across(d, t).wait_recv()
            self.sib_in[t, d] = self.sib_in[t, d] + own[d]

    def start(self):
        for u in range(SUBS):
            for d in range(2):
                self.hop(d, u, 0, True).start()

    def step(self, t):
        for u in range(SUBS):
            for d in range(2):
                into = self.land.at[t - 1, d, self.rows(u)]
                remote(into, into, self.rs.at[0, d, u, t - 1], self.rs.at[1, d, u, t - 1], self.ring.next[d]).wait_recv()
                self.land[t - 1, d, self.rows(u)] = self.land[t - 1, d, self.rows(u)] + self.sib_in[t, d, self.rows(u)]
                self.hop(d, u, t).start()

    def result(self, d):
        last = self.ring.n - 1
        for u in range(SUBS):
            into = self.land.at[last - 1, d, self.rows(u)]
            remote(
                into, into, self.rs.at[0, d, u, last - 1], self.rs.at[1, d, u, last - 1], self.ring.next[d]
            ).wait_recv()
        return self.land[last - 1, d] + self.sib_in[last, d]

    def finish(self):
        for u in range(SUBS):
            for d in range(2):
                self.hop(d, u, 0, True).wait_send()

        @pl.loop(1, self.ring.n - 1)
        def _(t):
            for u in range(SUBS):
                for d in range(2):
                    self.hop(d, u, t).wait_send()

        @pl.loop(0, self.ring.n)
        def _(t):
            for d in range(2):
                self.across(d, t).wait_send()


def columns(owner, slim):
    return pl.ds(pl.multiple_of(owner * slim, 128), slim)


def sums_kernel(n_rows, left_ref, factor_ref, cols_ref, dual_ref, fac, land, sib_in, sib_out, swap, load, rs, ss, xs):
    ring = Ring(n_rows)
    bulk = pltpu.make_async_copy(factor_ref, fac, load.at[0])
    bulk.start()
    ring.enter(True)
    bulk.wait()
    width = left_ref.shape[0] // 2
    slim = dual_ref.shape[1]

    def term(owner, d):
        return jnp.dot(
            left_ref[d * width : (d + 1) * width, :], fac[:, columns(owner, slim)], preferred_element_type=F32
        )

    sums = Scatter(ring, term, land, sib_in, sib_out, rs, ss)
    sums.prepare(0)
    sums.start()
    sums.prepare(1)

    @pl.loop(1, ring.n - 1)
    def _(t):
        sums.step(t)
        sums.prepare(t + 1)

    swap[0] = sums.result(0)
    move = remote(swap.at[0], swap.at[1], xs.at[0], xs.at[1], ring.partner)
    move.start()
    dual_ref[...] = sums.result(1)
    cols_ref[ring.rank] = swap[0]
    move.wait_recv()
    cols_ref[1 - ring.rank] = swap[1]
    move.wait_send()
    sums.finish()


def duals_kernel(n_rows, own_ref, core_ref, dual_ref, core, buf, acc, swap, load, rs, ss, xs):
    ring = Ring(n_rows)
    bulk = pltpu.make_async_copy(core_ref, core, load.at[0])
    bulk.start()
    buf[ring.row] = own_ref[...]
    acc[...] = jnp.zeros_like(acc)
    ring.enter(True)
    slim = own_ref.shape[1]
    gather = Gather(ring, buf, rs, ss)
    half = gather.half

    def consume(owner, d):
        pair = halves(buf[owner, d * half : (d + 1) * half, :])
        both = jnp.dot(pair, core[columns(owner, slim), :], preferred_element_type=F32)
        both = both[:half] + both[half:]
        for k in range(2):
            acc[k, d * half : (d + 1) * half, :] += both[:, k * slim : (k + 1) * slim]

    gather.step(0, first=True)
    bulk.wait()
    for d in range(2):
        consume(gather.mine(d, 0), d)

    @pl.loop(1, ring.n - 1)
    def _(t):
        gather.step(t)
        gather.wait_across(t - 1)
        for d in range(2):
            consume(gather.theirs(d, t - 1), d)
            consume(gather.mine(d, t), d)

    gather.step(ring.n - 1, last=True)
    gather.wait_across(ring.n - 2)
    for d in range(2):
        consume(gather.theirs(d, ring.n - 2), d)
        consume(gather.mine(d, ring.n - 1), d)
    gather.wait_across(ring.n - 1)
    for d in range(2):
        consume(gather.theirs(d, ring.n - 1), d)
    move = remote(acc.at[1 - ring.rank], swap, xs.at[0], xs.at[1], ring.partner)
    move.start()
    move.wait_recv()
    dual_ref[...] = acc[ring.rank] + swap[...]
    move.wait_send()
    gather.finish()


def weights_kernel(
    n_rows, cols_ref, own_ref, core_ref, duals_ref, weight_ref,
    core, buf, pairs, land, sib_in, sib_out, load, grs, gss, rs, ss,
):
    ring = Ring(n_rows)
    bulk = pltpu.make_async_copy(core_ref, core, load.at[0])
    bulk.start()
    buf[ring.row] = own_ref[...]
    slim = own_ref.shape[1]
    gather = Gather(ring, buf, grs, gss)
    half = gather.half
    for d in range(2):
        for k in range(2):
            pairs[d, :, k * slim : (k + 1) * slim] = halves(cols_ref[k, d * half : (d + 1) * half, :])
    ring.enter(False)
    gather.step(0, first=True)
    bulk.wait()

    def term(owner, d):
        both = lax.dot_general(pairs[d], core[columns(owner, slim), :], NT, preferred_element_type=F32)
        return both[:half] + both[half:]

    sums = Scatter(ring, term, land, sib_in, sib_out, rs, ss)
    sums.prepare(0)
    sums.start()
    sums.prepare(1)

    @pl.loop(1, ring.n - 1)
    def _(t):
        gather.step(t)
        sums.step(t)
        sums.prepare(t + 1)
        gather.wait_across(t - 1)

    gather.step(ring.n - 1, last=True)
    for d in range(2):
        weight_ref[d * half : (d + 1) * half, :] = sums.result(d)
    gather.wait_across(ring.n - 2)
    gather.wait_across(ring.n - 1)
    out = pltpu.make_async_copy(buf, duals_ref, load.at[1])
    out.start()
    gather.finish()
    sums.finish()
    out.wait()


def spread_kernel(
    n_rows, own_ref, duals_in, factor_ref, weights_ref, product_ref, fac, duals, buf, acc, swap, load, rs, ss, xs
):
    ring = Ring(n_rows)
    bulk = pltpu.make_async_copy(factor_ref, fac, load.at[0])
    bulk.start()
    second = pltpu.make_async_copy(duals_in, duals, load.at[1])
    second.start()
    buf[ring.row] = own_ref[...]
    acc[...] = jnp.zeros_like(acc)
    ring.enter(True)
    slim = own_ref.shape[1]
    width = own_ref.shape[0]
    gather = Gather(ring, buf, rs, ss)
    tiles = 4
    each = n_rows // tiles

    def multiply(first):
        @pl.loop(0, each)
        def _(i):
            owner = first * each + i
            both = lax.dot_general(
                fac[:, columns(owner, slim)], halves(duals[owner]), NT, preferred_element_type=F32
            )
            acc[...] += both[:, :width] + both[:, width:]

    gather.step(0, first=True)
    bulk.wait()
    second.wait()
    for i in range(tiles):
        multiply(i)
        if i + 1 < ring.n - 1:
            gather.step(i + 1)
    move = remote(acc, swap, xs.at[0], xs.at[1], ring.partner)
    move.start()

    @pl.loop(min(tiles + 1, ring.n - 1), ring.n - 1)
    def _(t):
        gather.step(t)

    gather.step(ring.n - 1, last=True)

    @pl.loop(0, ring.n)
    def _(t):
        gather.wait_across(t)

    out = pltpu.make_async_copy(buf, weights_ref, load.at[2])
    out.start()
    move.wait_recv()
    product_ref[...] = acc[...] + swap[...]
    move.wait_send()
    gather.finish()
    out.wait()


def outer_kernel(scale_ref, left_ref, rank_ref, weights_ref, duals_ref, out_ref):
    first = lax.axis_index("rank") * (out_ref.shape[1] * pl.num_programs(0)) + pl.program_id(0) * out_ref.shape[1]
    right = halves(jnp.concatenate([weights_ref[0], duals_ref[0]], axis=0))
    scale = scale_ref[0]
    rows = left_ref.shape[0]
    tile = min(rows, 256)
    for r in range(0, rows, tile):
        total = jnp.dot(left_ref[r : r + tile, :], right, preferred_element_type=F32)
        where = first + lax.broadcasted_iota(jnp.int32, total.shape, 1)
        keep = where <= rank_ref[r : r + tile, :]
        out_ref[r : r + tile, :] = jnp.where(keep, -total / scale, 0.0).astype(BF16)


def sems(*shape):
    return pltpu.SemaphoreType.DMA(shape)


def params(n):
    return pltpu.CompilerParams(collective_id=n, has_side_effects=True, vmem_limit_bytes=60 * 2**20)


def shape_of(*shape):
    return jax.ShapeDtypeStruct(shape, F32)


def ranks_of_rows(pivots, first_row, rows_dev):
    total = pivots.shape[0]
    local = pivots - first_row
    number = jnp.arange(1, total + 1, dtype=jnp.int32)
    high = (local >> 7)[None, :] == jnp.arange(rows_dev // 128, dtype=jnp.int32)[:, None]
    low = ((local & 127)[:, None] == jnp.arange(128, dtype=jnp.int32)[None, :]).astype(BF16)
    upper = jnp.where(high, number >> 7, 0).astype(BF16)
    lower = jnp.where(high, number & 127, 0).astype(BF16)
    found = jnp.dot(jnp.concatenate([upper, lower], axis=0), low, preferred_element_type=F32)
    found = found.astype(jnp.int32).reshape(2, rows_dev)
    found = found[0] * 128 + found[1]
    return jnp.where(found > 0, found - 1, total)


def ring_body(factor, probes, cotangent, core_inverse, pivots, noise):
    rows_dev, block_cols = factor.shape
    width = probes.shape[1]
    n_rows = lax.axis_size("rows")
    slim = block_cols // n_rows
    n = n_rows // 2
    half = width // 2
    scale = noise[0]
    core_tile = core_inverse.reshape(block_cols, 2 * slim)
    left = jnp.concatenate([probes.T, cotangent.T], axis=0)
    ring_sem = sems(2, 2, SUBS, n)
    sib_sem = sems(2, 2, n)
    bucket = pltpu.VMEM((n_rows, width, slim), F32)
    coef_cols, dual_in = pl.pallas_call(
        functools.partial(sums_kernel, n_rows),
        out_shape=(shape_of(2, width, slim), shape_of(width, slim)),
        in_specs=[VMEM, ANY],
        out_specs=(VMEM, VMEM),
        scratch_shapes=[
            pltpu.VMEM(factor.shape, BF16),
            pltpu.VMEM((n - 1, 2, width, slim), F32),
            pltpu.VMEM((n, 2, width, slim), F32),
            pltpu.VMEM((n, 2, width, slim), F32),
            pltpu.VMEM((2, width, slim), F32),
            sems(1), ring_sem, sib_sem, sems(2),
        ],
        compiler_params=params(0),
        name="sums",
    )(left, factor)
    dual_own = pl.pallas_call(
        functools.partial(duals_kernel, n_rows),
        out_shape=shape_of(width, slim),
        in_specs=[VMEM, ANY],
        out_specs=VMEM,
        scratch_shapes=[
            pltpu.VMEM(core_tile.shape, BF16),
            bucket,
            pltpu.VMEM((2, width, slim), F32),
            pltpu.VMEM((width, slim), F32),
            sems(1), ring_sem, ring_sem, sems(2),
        ],
        compiler_params=params(1),
        name="duals",
    )(dual_in, core_tile)
    duals, weight_own = pl.pallas_call(
        functools.partial(weights_kernel, n_rows),
        out_shape=(shape_of(n_rows, width, slim), shape_of(width, slim)),
        in_specs=[VMEM, VMEM, ANY],
        out_specs=(ANY, VMEM),
        scratch_shapes=[
            pltpu.VMEM(core_tile.shape, BF16),
            bucket,
            pltpu.VMEM((2, width, 2 * slim), BF16),
            pltpu.VMEM((n - 1, 2, half, slim), F32),
            pltpu.VMEM((n, 2, half, slim), F32),
            pltpu.VMEM((n, 2, half, slim), F32),
            sems(2), ring_sem, ring_sem, ring_sem, sib_sem,
        ],
        compiler_params=params(2),
        name="weights",
    )(coef_cols, dual_own, core_tile)
    weights, product = pl.pallas_call(
        functools.partial(spread_kernel, n_rows),
        out_shape=(shape_of(n_rows, width, slim), shape_of(rows_dev, width)),
        in_specs=[VMEM, ANY, ANY],
        out_specs=(ANY, VMEM),
        scratch_shapes=[
            pltpu.VMEM(factor.shape, BF16),
            bucket,
            bucket,
            pltpu.VMEM((rows_dev, width), F32),
            pltpu.VMEM((rows_dev, width), F32),
            sems(3), ring_sem, ring_sem, sems(2),
        ],
        compiler_params=params(3),
        name="spread",
    )(weight_own, duals, factor)
    probe_grad = ((cotangent.astype(F32) - product) / scale).astype(BF16)
    pivot_rank = ranks_of_rows(pivots, lax.axis_index("rows") * rows_dev, rows_dev)
    pair = jnp.concatenate([cotangent, probes, cotangent, probes], axis=1)
    block = pl.BlockSpec((1, width, slim), lambda j: (j, 0, 0))
    grads = pl.pallas_call(
        outer_kernel,
        grid=(n_rows,),
        out_shape=jax.ShapeDtypeStruct(factor.shape, BF16),
        in_specs=[
            pl.BlockSpec(memory_space=pltpu.SMEM),
            pl.BlockSpec((rows_dev, 4 * width), lambda j: (0, 0)),
            pl.BlockSpec((rows_dev, 1), lambda j: (0, 0)),
            block,
            block,
        ],
        out_specs=pl.BlockSpec((rows_dev, slim), lambda j: (0, j)),
        compiler_params=pltpu.CompilerParams(vmem_limit_bytes=40 * 2**20),
        name="outer",
    )(noise, pair, pivot_rank[:, None], weights, duals)
    return probe_grad, grads


def body(factor, probes, cotangent, core_inverse, pivots, noise):
    highest = lax.Precision.HIGHEST
    rows_dev = factor.shape[0]
    block_cols = factor.shape[1]
    width = probes.shape[1]
    n_rows = lax.axis_size("rows")
    n_rank = lax.axis_size("rank")
    slim = block_cols // n_rows
    row_index = lax.axis_index("rows")
    rank_index = lax.axis_index("rank")
    scale = noise[0]
    core_tile = core_inverse.reshape(block_cols, n_rank * slim).astype(jnp.float32)
    contract = (((0,), (0,)), ((), ()))
    stacked = jnp.concatenate([probes, cotangent], axis=1)
    partial_sums = lax.dot_general(factor, stacked, contract, preferred_element_type=jnp.float32)
    share = lax.psum_scatter(partial_sums, "rows", scatter_dimension=0, tiled=True)
    coef_part = share[:, :width]
    dual_full = lax.all_gather(share[:, width:], "rows", axis=0, tiled=True)
    coef_cols = lax.all_gather(coef_part, "rank", axis=0, tiled=True)
    weights_blk = lax.psum(
        jnp.dot(core_tile, coef_cols, precision=highest, preferred_element_type=jnp.float32), "rows"
    )
    dual_part = lax.psum_scatter(
        lax.dot_general(
            core_tile, dual_full, contract, precision=highest, preferred_element_type=jnp.float32
        ),
        "rank",
        scatter_dimension=0,
        tiled=True,
    )
    duals_blk = lax.all_gather(dual_part, "rows", axis=0, tiled=True)
    local_product = jnp.dot(
        factor.astype(jnp.float32), duals_blk, precision=highest, preferred_element_type=jnp.float32
    )
    correction = lax.psum(local_product, "rank")
    probe_grad = ((cotangent.astype(jnp.float32) - correction) / scale).astype(jnp.bfloat16)
    left_side = jnp.concatenate([cotangent, probes], axis=1).astype(jnp.float32)
    right_side = jnp.concatenate([weights_blk, duals_blk], axis=1)
    outer_sum = lax.dot_general(
        left_side,
        right_side,
        (((1,), (1,)), ((), ())),
        precision=highest,
        preferred_element_type=jnp.float32,
    )
    grads = -outer_sum / scale
    local_rows = pivots - row_index * rows_dev
    inside = (local_rows >= 0) & (local_rows < rows_dev)
    target = jnp.where(inside, local_rows, rows_dev)
    total_rank = pivots.shape[0]
    pivot_rank = (
        jnp.full((rows_dev + 1,), total_rank, jnp.int32)
        .at[target]
        .set(jnp.arange(total_rank, dtype=jnp.int32))[:rows_dev]
    )
    columns = rank_index * block_cols + jnp.arange(block_cols, dtype=jnp.int32)
    grads = jnp.where(columns[None, :] > pivot_rank[:, None], jnp.float32(0.0), grads)
    return (probe_grad, grads.astype(jnp.bfloat16))


def solution(mesh):
    placed = (
        P("rows", "rank"),
        P("rows", None),
        P("rows", None),
        P("rank", None, "rows"),
        P(),
        P(),
    )
    n_rows, n_rank = mesh.shape["rows"], mesh.shape["rank"]

    def chosen(factor, probes, cotangent, core_inverse, pivots, noise):
        slim = factor.shape[1] // n_rows
        fits = n_rank == 2 and n_rows % 4 == 0 and slim % 128 == 0 and factor.shape[0] % 128 == 0
        run = ring_body if fits and pivots.shape[0] <= 2**15 else body
        return run(factor, probes, cotangent, core_inverse, pivots, noise)

    return jax.shard_map(
        chosen,
        mesh=mesh,
        in_specs=placed,
        out_specs=(P("rows", None), P("rows", "rank")),
        check_vma=False,
    )
```

```python
import functools

import jax
import jax.numpy as jnp
from jax import lax
from jax.experimental import pallas as pl
from jax.experimental.pallas import tpu as pltpu
from jax.sharding import PartitionSpec as P

MESH = pl.DeviceIdType.MESH
VMEM = pl.BlockSpec(memory_space=pltpu.VMEM)
ANY = pl.BlockSpec(memory_space=pl.ANY)
F32 = jnp.float32
BF16 = jnp.bfloat16
SUBS = 2
NT = (((1,), (1,)), ((), ()))


def halves(x):
    high = x.astype(BF16)
    low = (x - high.astype(F32)).astype(BF16)
    return jnp.concatenate([high, low], axis=0)


class Ring:
    def __init__(self, n_rows):
        self.n = n_rows // 2
        row = lax.axis_index("rows")
        self.row = row
        self.rank = lax.axis_index("rank")
        self.core = row % 2
        chip = row // 2
        odd = chip % 2
        self.pos = (1 - odd) * (chip // 2) + odd * (self.n - 1 - chip // 2)
        self.next = [self.device(self.pos + 1), self.device(self.pos - 1)]
        self.sibling = (self.owner(self.pos, True), self.rank)
        self.partner = (row, 1 - self.rank)

    def owner(self, pos, other=False):
        pos = (pos + 2 * self.n) % self.n
        upper = (2 * pos) // self.n
        chip = (1 - upper) * (2 * pos) + upper * (2 * (self.n - 1 - pos) + 1)
        core = (1 - self.core) if other else self.core
        return 2 * chip + core

    def device(self, pos):
        return (self.owner(pos), self.rank)

    def enter(self, with_partner):
        barrier = pltpu.get_barrier_semaphore()
        peers = self.next + [self.sibling] + ([self.partner] if with_partner else [])
        for peer in peers:
            pl.semaphore_signal(barrier, inc=1, device_id=peer, device_id_type=MESH)
        pl.semaphore_wait(barrier, len(peers))


def remote(src, dst, send, recv, device):
    return pltpu.make_async_remote_copy(
        src_ref=src, dst_ref=dst, send_sem=send, recv_sem=recv, device_id=device, device_id_type=MESH
    )


class Gather:
    def __init__(self, ring, buf, ring_sems, sib_sems):
        self.ring, self.buf = ring, buf
        self.rs, self.ss = ring_sems, sib_sems
        self.half = buf.shape[1] // 2
        self.sub = self.half // SUBS

    def at(self, d, t):
        return self.ring.pos - t if d == 0 else self.ring.pos + t

    def part(self, owner, d, u):
        return self.buf.at[owner, pl.ds(d * self.half + u * self.sub, self.sub)]

    def hop(self, d, u, t):
        ref = self.part(self.ring.owner(self.at(d, t)), d, u)
        return remote(ref, ref, self.rs.at[0, d, u, t], self.rs.at[1, d, u, t], self.ring.next[d])

    def hop_in(self, d, u, t):
        ref = self.part(self.ring.owner(self.at(d, t + 1)), d, u)
        return remote(ref, ref, self.rs.at[0, d, u, t], self.rs.at[1, d, u, t], self.ring.next[d])

    def across(self, d, u, t):
        ref = self.part(self.ring.owner(self.at(d, t)), d, u)
        return remote(ref, ref, self.ss.at[0, d, u, t], self.ss.at[1, d, u, t], self.ring.sibling)

    def across_in(self, d, u, t):
        ref = self.part(self.ring.owner(self.at(d, t), True), d, u)
        return remote(ref, ref, self.ss.at[0, d, u, t], self.ss.at[1, d, u, t], self.ring.sibling)

    def step(self, t, first=False, last=False):
        for u in range(SUBS):
            for d in range(2):
                if not first:
                    self.hop_in(d, u, t - 1).wait_recv()
                if not last:
                    self.hop(d, u, t).start()
                self.across(d, u, t).start()

    def wait_across(self, t):
        for u in range(SUBS):
            for d in range(2):
                self.across_in(d, u, t).wait_recv()

    def mine(self, d, t):
        return self.ring.owner(self.at(d, t))

    def theirs(self, d, t):
        return self.ring.owner(self.at(d, t), True)

    def finish(self):
        @pl.loop(0, self.ring.n)
        def _(t):
            for u in range(SUBS):
                for d in range(2):
                    self.across(d, u, t).wait_send()

        @pl.loop(0, self.ring.n - 1)
        def _(t):
            for u in range(SUBS):
                for d in range(2):
                    self.hop(d, u, t).wait_send()


class Scatter:
    def __init__(self, ring, term, land, sib_in, sib_out, ring_sems, sib_sems):
        self.ring, self.term = ring, term
        self.land, self.sib_in, self.sib_out = land, sib_in, sib_out
        self.rs, self.ss = ring_sems, sib_sems
        self.sub = land.shape[2] // SUBS

    def at(self, d, t):
        return self.ring.pos - 1 - t if d == 0 else self.ring.pos + 1 + t

    def across(self, d, t):
        return remote(
            self.sib_out.at[t, d], self.sib_in.at[t, d], self.ss.at[0, d, t], self.ss.at[1, d, t], self.ring.sibling
        )

    def rows(self, u):
        return pl.ds(u * self.sub, self.sub)

    def hop(self, d, u, t, first=False):
        src = self.sib_in.at[0, d, self.rows(u)] if first else self.land.at[t - 1, d, self.rows(u)]
        dst = self.land.at[t, d, self.rows(u)]
        return remote(src, dst, self.rs.at[0, d, u, t], self.rs.at[1, d, u, t], self.ring.next[d])

    def prepare(self, t):
        for d in range(2):
            self.sib_out[t, d] = self.term(self.ring.owner(self.at(d, t), True), d)
            self.across(d, t).start()
        own = [self.term(self.ring.owner(self.at(d, t)), d) for d in range(2)]
        for d in range(2):
            self.across(d, t).wait_recv()
            self.sib_in[t, d] = self.sib_in[t, d] + own[d]

    def start(self):
        for u in range(SUBS):
            for d in range(2):
                self.hop(d, u, 0, True).start()

    def step(self, t):
        for u in range(SUBS):
            for d in range(2):
                into = self.land.at[t - 1, d, self.rows(u)]
                remote(into, into, self.rs.at[0, d, u, t - 1], self.rs.at[1, d, u, t - 1], self.ring.next[d]).wait_recv()
                self.land[t - 1, d, self.rows(u)] = self.land[t - 1, d, self.rows(u)] + self.sib_in[t, d, self.rows(u)]
                self.hop(d, u, t).start()

    def result(self, d):
        last = self.ring.n - 1
        for u in range(SUBS):
            into = self.land.at[last - 1, d, self.rows(u)]
            remote(
                into, into, self.rs.at[0, d, u, last - 1], self.rs.at[1, d, u, last - 1], self.ring.next[d]
            ).wait_recv()
        return self.land[last - 1, d] + self.sib_in[last, d]

    def finish(self):
        for u in range(SUBS):
            for d in range(2):
                self.hop(d, u, 0, True).wait_send()

        @pl.loop(1, self.ring.n - 1)
        def _(t):
            for u in range(SUBS):
                for d in range(2):
                    self.hop(d, u, t).wait_send()

        @pl.loop(0, self.ring.n)
        def _(t):
            for d in range(2):
                self.across(d, t).wait_send()


def columns(owner, slim):
    return pl.ds(pl.multiple_of(owner * slim, 128), slim)


def sums_kernel(
    n_rows, left_ref, factor_ref, core_ref, coef_ref, dual_ref, tile_ref,
    fac, land, sib_in, sib_out, raw, flat, load, raws, flats, rs, ss,
):
    ring = Ring(n_rows)
    slim = dual_ref.shape[1]
    width = dual_ref.shape[0]
    n = ring.n
    deep = raw.shape[1]

    def piece(offset, slot):
        chip = ring.owner(ring.pos + offset) // 2
        cols = columns(chip, 2 * slim)
        return pltpu.make_async_copy(factor_ref.at[:, cols], fac.at[:, cols], load.at[slot])

    order = [-1, 1] + [o for i in range(2, n // 2) for o in (-i, i)] + [n // 2, 0]
    pieces = [piece(offset, slot) for slot, offset in enumerate(order)]
    for copy in pieces:
        copy.start()

    def fetch(t):
        rows = pl.ds(pl.multiple_of(t * deep, 16), deep)
        return pltpu.make_async_copy(core_ref.at[rows], raw.at[t % 2], raws.at[t % 2])

    def keep(t):
        rows = pl.ds(pl.multiple_of(t * deep, 16), deep)
        return pltpu.make_async_copy(flat.at[t % 2], tile_ref.at[rows], flats.at[t % 2])

    def flatten(t, first=False, last=False):
        fetch(t).wait()
        if not last:
            fetch(t + 1).start()
        if not first:
            keep(t - 1).wait()

        @pl.loop(0, deep // 32)
        def _(i):
            rows = pl.ds(pl.multiple_of(i * 32, 32), 32)
            for k in range(2):
                flat[t % 2, rows, k * slim : (k + 1) * slim] = raw[t % 2, rows, k, :]

        keep(t).start()

    fetch(0).start()
    ring.enter(False)

    def term(owner, d):
        return jnp.dot(
            left_ref[d * width : (d + 1) * width, :], fac[:, columns(owner, slim)], preferred_element_type=F32
        )

    sums = Scatter(ring, term, land, sib_in, sib_out, rs, ss)
    pieces[0].wait()
    pieces[1].wait()
    sums.prepare(0)
    sums.start()
    for copy in pieces[2:]:
        copy.wait()
    sums.prepare(1)
    flatten(0, first=True)

    @pl.loop(1, n - 1)
    def _(t):
        sums.step(t)
        sums.prepare(t + 1)
        flatten(t)

    flatten(n - 1, last=True)
    coef_ref[...] = sums.result(0)
    dual_ref[...] = sums.result(1)
    keep(n - 1).wait()
    sums.finish()


def mix_kernel(
    n_rows, coef_ref, own_ref, core_ref, dual_ref, weight_ref,
    core, buf, acc, swap, coefs, pairs, land, sib_in, sib_out, load, grs, gss, rs, ss, xs,
):
    ring = Ring(n_rows)
    bulk = pltpu.make_async_copy(core_ref, core, load.at[0])
    bulk.start()
    buf[ring.row] = own_ref[...]
    acc[...] = jnp.zeros_like(acc)
    slim = own_ref.shape[1]
    gather = Gather(ring, buf, grs, gss)
    half = gather.half

    def consume(owner, d):
        pair = halves(buf[owner, d * half : (d + 1) * half, :])
        both = jnp.dot(pair, core[columns(owner, slim), :], preferred_element_type=F32)
        both = both[:half] + both[half:]
        for k in range(2):
            acc[k, d * half : (d + 1) * half, :] += both[:, k * slim : (k + 1) * slim]

    def term(owner, d):
        rows = columns(owner, slim)
        both = lax.dot_general(pairs[0, d], core[rows, :slim], NT, preferred_element_type=F32)
        both = both + lax.dot_general(pairs[1, d], core[rows, slim:], NT, preferred_element_type=F32)
        return both[:half] + both[half:]

    ring.enter(True)
    other = remote(coef_ref, coefs, xs.at[0], xs.at[1], ring.partner)
    other.start()
    gather.step(0, first=True)
    for d in range(2):
        pairs[ring.rank, d] = halves(coef_ref[d * half : (d + 1) * half, :])
    bulk.wait()
    for d in range(2):
        consume(gather.mine(d, 0), d)
    other.wait_recv()
    for d in range(2):
        pairs[1 - ring.rank, d] = halves(coefs[d * half : (d + 1) * half, :])
    sums = Scatter(ring, term, land, sib_in, sib_out, rs, ss)
    sums.prepare(0)
    sums.start()
    sums.prepare(1)

    @pl.loop(1, ring.n - 1)
    def _(t):
        gather.step(t)
        sums.step(t)
        sums.prepare(t + 1)
        gather.wait_across(t - 1)
        for d in range(2):
            consume(gather.theirs(d, t - 1), d)
            consume(gather.mine(d, t), d)

    gather.step(ring.n - 1, last=True)
    gather.wait_across(ring.n - 2)
    for d in range(2):
        consume(gather.theirs(d, ring.n - 2), d)
        consume(gather.mine(d, ring.n - 1), d)
    gather.wait_across(ring.n - 1)
    for d in range(2):
        consume(gather.theirs(d, ring.n - 1), d)
    move = remote(acc.at[1 - ring.rank], swap, xs.at[2], xs.at[3], ring.partner)
    move.start()
    for d in range(2):
        weight_ref[d * half : (d + 1) * half, :] = sums.result(d)
    move.wait_recv()
    dual_ref[...] = acc[ring.rank] + swap[...]
    move.wait_send()
    other.wait_send()
    gather.finish()
    sums.finish()


def spread_kernel(
    n_rows, dual_ref, weight_ref, factor_ref, duals_ref, weights_ref, product_ref,
    fac, dbuf, wbuf, load, outs, drs, dss, wrs, wss,
):
    ring = Ring(n_rows)
    bulk = pltpu.make_async_copy(factor_ref, fac, load.at[0])
    bulk.start()
    dbuf[ring.row] = dual_ref[...]
    wbuf[ring.row] = weight_ref[...]
    product_ref[...] = jnp.zeros_like(product_ref)
    slim = dual_ref.shape[1]
    duals = Gather(ring, dbuf, drs, dss)
    weights = Gather(ring, wbuf, wrs, wss)
    half = duals.half

    def out(which, other, d, t):
        buf, ref = ((dbuf, duals_ref), (wbuf, weights_ref))[which]
        owner = duals.theirs(d, t) if other else duals.mine(d, t)
        rows = pl.ds(d * half, half)
        return pltpu.make_async_copy(buf.at[owner, rows], ref.at[owner, rows], outs.at[which, other, d, t])

    def consume(owner, d):
        right = halves(dbuf[owner, d * half : (d + 1) * half, :])
        both = lax.dot_general(fac[:, columns(owner, slim)], right, NT, preferred_element_type=F32)
        product_ref[:, d * half : (d + 1) * half] += both[:, :half] + both[:, half:]

    def use(other, t):
        for d in range(2):
            out(0, other, d, t).start()
            out(1, other, d, t).start()
        for d in range(2):
            consume(duals.theirs(d, t) if other else duals.mine(d, t), d)

    def crossed(t):
        duals.wait_across(t)
        weights.wait_across(t)

    ring.enter(False)
    duals.step(0, first=True)
    weights.step(0, first=True)
    bulk.wait()
    use(0, 0)

    @pl.loop(1, ring.n - 1)
    def _(t):
        duals.step(t)
        weights.step(t)
        crossed(t - 1)
        use(1, t - 1)
        use(0, t)

    duals.step(ring.n - 1, last=True)
    weights.step(ring.n - 1, last=True)
    crossed(ring.n - 2)
    use(1, ring.n - 2)
    use(0, ring.n - 1)
    crossed(ring.n - 1)
    use(1, ring.n - 1)

    @pl.loop(0, ring.n)
    def _(t):
        for which in range(2):
            for other in range(2):
                for d in range(2):
                    out(which, other, d, t).wait()

    duals.finish()
    weights.finish()


def outer_kernel(scale_ref, left_ref, rank_ref, weights_ref, duals_ref, out_ref):
    first = lax.axis_index("rank") * (out_ref.shape[1] * pl.num_programs(0)) + pl.program_id(0) * out_ref.shape[1]
    right = halves(jnp.concatenate([weights_ref[0], duals_ref[0]], axis=0))
    scale = scale_ref[0]
    rows = left_ref.shape[0]
    tile = min(rows, 256)
    for r in range(0, rows, tile):
        total = jnp.dot(left_ref[r : r + tile, :], right, preferred_element_type=F32)
        where = first + lax.broadcasted_iota(jnp.int32, total.shape, 1)
        keep = where <= rank_ref[r : r + tile, :]
        out_ref[r : r + tile, :] = jnp.where(keep, -total / scale, 0.0).astype(BF16)


def sems(*shape):
    return pltpu.SemaphoreType.DMA(shape)


def params(n):
    return pltpu.CompilerParams(collective_id=n, has_side_effects=True, vmem_limit_bytes=60 * 2**20)


def shape_of(*shape):
    return jax.ShapeDtypeStruct(shape, F32)


def ranks_of_rows(pivots, first_row, rows_dev):
    total = pivots.shape[0]
    local = pivots - first_row
    number = jnp.arange(1, total + 1, dtype=jnp.int32)
    high = (local >> 7)[None, :] == jnp.arange(rows_dev // 128, dtype=jnp.int32)[:, None]
    low = ((local & 127)[:, None] == jnp.arange(128, dtype=jnp.int32)[None, :]).astype(BF16)
    upper = jnp.where(high, number >> 7, 0).astype(BF16)
    lower = jnp.where(high, number & 127, 0).astype(BF16)
    found = jnp.dot(jnp.concatenate([upper, lower], axis=0), low, preferred_element_type=F32)
    found = found.astype(jnp.int32).reshape(2, rows_dev)
    found = found[0] * 128 + found[1]
    return jnp.where(found > 0, found - 1, total)


def ring_body(factor, probes, cotangent, core_inverse, pivots, noise):
    rows_dev, block_cols = factor.shape
    width = probes.shape[1]
    n_rows = lax.axis_size("rows")
    slim = block_cols // n_rows
    n = n_rows // 2
    half = width // 2
    scale = noise[0]
    left = jnp.concatenate([probes.T, cotangent.T], axis=0)
    deep = block_cols // n
    ring_sem = sems(2, 2, SUBS, n)
    sib_sem = sems(2, 2, n)
    bucket = pltpu.VMEM((n_rows, width, slim), F32)
    block = pltpu.VMEM((width, slim), F32)
    coef_own, dual_in, core_tile = pl.pallas_call(
        functools.partial(sums_kernel, n_rows),
        out_shape=(
            shape_of(width, slim),
            shape_of(width, slim),
            jax.ShapeDtypeStruct((block_cols, 2 * slim), BF16),
        ),
        in_specs=[VMEM, ANY, ANY],
        out_specs=(VMEM, VMEM, ANY),
        scratch_shapes=[
            pltpu.VMEM(factor.shape, BF16),
            pltpu.VMEM((n - 1, 2, width, slim), F32),
            pltpu.VMEM((n, 2, width, slim), F32),
            pltpu.VMEM((n, 2, width, slim), F32),
            pltpu.VMEM((2, deep, 2, slim), BF16),
            pltpu.VMEM((2, deep, 2 * slim), BF16),
            sems(n), sems(2), sems(2), ring_sem, sib_sem,
        ],
        compiler_params=params(0),
        name="sums",
    )(left, factor, core_inverse)
    dual_own, weight_own = pl.pallas_call(
        functools.partial(mix_kernel, n_rows),
        out_shape=(shape_of(width, slim), shape_of(width, slim)),
        in_specs=[VMEM, VMEM, ANY],
        out_specs=(VMEM, VMEM),
        scratch_shapes=[
            pltpu.VMEM(core_tile.shape, BF16),
            bucket,
            pltpu.VMEM((2, width, slim), F32),
            block,
            block,
            pltpu.VMEM((2, 2, width, slim), BF16),
            pltpu.VMEM((n - 1, 2, half, slim), F32),
            pltpu.VMEM((n, 2, half, slim), F32),
            pltpu.VMEM((n, 2, half, slim), F32),
            sems(1), ring_sem, ring_sem, ring_sem, sib_sem, sems(4),
        ],
        compiler_params=params(1),
        name="mix",
    )(coef_own, dual_in, core_tile)
    duals, weights, product = pl.pallas_call(
        functools.partial(spread_kernel, n_rows),
        out_shape=(shape_of(n_rows, width, slim), shape_of(n_rows, width, slim), shape_of(rows_dev, width)),
        in_specs=[VMEM, VMEM, ANY],
        out_specs=(ANY, ANY, VMEM),
        scratch_shapes=[
            pltpu.VMEM(factor.shape, BF16),
            bucket,
            bucket,
            sems(1), sems(2, 2, 2, n), ring_sem, ring_sem, ring_sem, ring_sem,
        ],
        compiler_params=params(2),
        name="spread",
    )(dual_own, weight_own, factor)
    product = product + lax.ppermute(product, "rank", [(0, 1), (1, 0)])
    probe_grad = ((cotangent.astype(F32) - product) / scale).astype(BF16)
    pivot_rank = ranks_of_rows(pivots, lax.axis_index("rows") * rows_dev, rows_dev)
    pair = jnp.concatenate([cotangent, probes, cotangent, probes], axis=1)
    block = pl.BlockSpec((1, width, slim), lambda j: (j, 0, 0))
    grads = pl.pallas_call(
        outer_kernel,
        grid=(n_rows,),
        out_shape=jax.ShapeDtypeStruct(factor.shape, BF16),
        in_specs=[
            pl.BlockSpec(memory_space=pltpu.SMEM),
            pl.BlockSpec((rows_dev, 4 * width), lambda j: (0, 0)),
            pl.BlockSpec((rows_dev, 1), lambda j: (0, 0)),
            block,
            block,
        ],
        out_specs=pl.BlockSpec((rows_dev, slim), lambda j: (0, j)),
        compiler_params=pltpu.CompilerParams(vmem_limit_bytes=60 * 2**20),
        cost_estimate=pl.CostEstimate(
            flops=8 * rows_dev * width * block_cols,
            bytes_accessed=2 * rows_dev * block_cols + 8 * width * block_cols,
            transcendentals=0,
        ),
        name="outer",
    )(noise, pair, pivot_rank[:, None], weights, duals)
    return probe_grad, grads


def body(factor, probes, cotangent, core_inverse, pivots, noise):
    highest = lax.Precision.HIGHEST
    rows_dev = factor.shape[0]
    block_cols = factor.shape[1]
    width = probes.shape[1]
    n_rows = lax.axis_size("rows")
    n_rank = lax.axis_size("rank")
    slim = block_cols // n_rows
    row_index = lax.axis_index("rows")
    rank_index = lax.axis_index("rank")
    scale = noise[0]
    core_tile = core_inverse.reshape(block_cols, n_rank * slim).astype(jnp.float32)
    contract = (((0,), (0,)), ((), ()))
    stacked = jnp.concatenate([probes, cotangent], axis=1)
    partial_sums = lax.dot_general(factor, stacked, contract, preferred_element_type=jnp.float32)
    share = lax.psum_scatter(partial_sums, "rows", scatter_dimension=0, tiled=True)
    coef_part = share[:, :width]
    dual_full = lax.all_gather(share[:, width:], "rows", axis=0, tiled=True)
    coef_cols = lax.all_gather(coef_part, "rank", axis=0, tiled=True)
    weights_blk = lax.psum(
        jnp.dot(core_tile, coef_cols, precision=highest, preferred_element_type=jnp.float32), "rows"
    )
    dual_part = lax.psum_scatter(
        lax.dot_general(
            core_tile, dual_full, contract, precision=highest, preferred_element_type=jnp.float32
        ),
        "rank",
        scatter_dimension=0,
        tiled=True,
    )
    duals_blk = lax.all_gather(dual_part, "rows", axis=0, tiled=True)
    local_product = jnp.dot(
        factor.astype(jnp.float32), duals_blk, precision=highest, preferred_element_type=jnp.float32
    )
    correction = lax.psum(local_product, "rank")
    probe_grad = ((cotangent.astype(jnp.float32) - correction) / scale).astype(jnp.bfloat16)
    left_side = jnp.concatenate([cotangent, probes], axis=1).astype(jnp.float32)
    right_side = jnp.concatenate([weights_blk, duals_blk], axis=1)
    outer_sum = lax.dot_general(
        left_side,
        right_side,
        (((1,), (1,)), ((), ())),
        precision=highest,
        preferred_element_type=jnp.float32,
    )
    grads = -outer_sum / scale
    local_rows = pivots - row_index * rows_dev
    inside = (local_rows >= 0) & (local_rows < rows_dev)
    target = jnp.where(inside, local_rows, rows_dev)
    total_rank = pivots.shape[0]
    pivot_rank = (
        jnp.full((rows_dev + 1,), total_rank, jnp.int32)
        .at[target]
        .set(jnp.arange(total_rank, dtype=jnp.int32))[:rows_dev]
    )
    columns = rank_index * block_cols + jnp.arange(block_cols, dtype=jnp.int32)
    grads = jnp.where(columns[None, :] > pivot_rank[:, None], jnp.float32(0.0), grads)
    return (probe_grad, grads.astype(jnp.bfloat16))


def solution(mesh):
    placed = (
        P("rows", "rank"),
        P("rows", None),
        P("rows", None),
        P("rank", None, "rows"),
        P(),
        P(),
    )
    n_rows, n_rank = mesh.shape["rows"], mesh.shape["rank"]

    def chosen(factor, probes, cotangent, core_inverse, pivots, noise):
        slim = factor.shape[1] // n_rows
        fits = n_rank == 2 and n_rows % 4 == 0 and n_rows >= 8 and slim % 128 == 0 and factor.shape[0] % 128 == 0
        run = ring_body if fits and pivots.shape[0] <= 2**15 else body
        return run(factor, probes, cotangent, core_inverse, pivots, noise)

    return jax.shard_map(
        chosen,
        mesh=mesh,
        in_specs=placed,
        out_specs=(P("rows", None), P("rows", "rank")),
        check_vma=False,
    )
```

```python
import functools

import jax
import jax.numpy as jnp
from jax import lax
from jax.experimental import pallas as pl
from jax.experimental.pallas import tpu as pltpu
from jax.sharding import PartitionSpec as P

MESH = pl.DeviceIdType.MESH
VMEM = pl.BlockSpec(memory_space=pltpu.VMEM)
ANY = pl.BlockSpec(memory_space=pl.ANY)
F32 = jnp.float32
BF16 = jnp.bfloat16
SUBS = 2
NT = (((1,), (1,)), ((), ()))


def halves(x):
    high = x.astype(BF16)
    low = (x - high.astype(F32)).astype(BF16)
    return jnp.concatenate([high, low], axis=0)


class Ring:
    def __init__(self, n_rows):
        self.n = n_rows // 2
        row = lax.axis_index("rows")
        self.row = row
        self.rank = lax.axis_index("rank")
        self.core = row % 2
        chip = row // 2
        odd = chip % 2
        self.pos = (1 - odd) * (chip // 2) + odd * (self.n - 1 - chip // 2)
        self.next = [self.device(self.pos + 1), self.device(self.pos - 1)]
        self.sibling = (self.owner(self.pos, True), self.rank)
        self.partner = (row, 1 - self.rank)

    def owner(self, pos, other=False):
        pos = (pos + 2 * self.n) % self.n
        upper = (2 * pos) // self.n
        chip = (1 - upper) * (2 * pos) + upper * (2 * (self.n - 1 - pos) + 1)
        core = (1 - self.core) if other else self.core
        return 2 * chip + core

    def device(self, pos):
        return (self.owner(pos), self.rank)

    def enter(self, with_partner):
        barrier = pltpu.get_barrier_semaphore()
        peers = self.next + [self.sibling] + ([self.partner] if with_partner else [])
        for peer in peers:
            pl.semaphore_signal(barrier, inc=1, device_id=peer, device_id_type=MESH)
        pl.semaphore_wait(barrier, len(peers))


def remote(src, dst, send, recv, device):
    return pltpu.make_async_remote_copy(
        src_ref=src, dst_ref=dst, send_sem=send, recv_sem=recv, device_id=device, device_id_type=MESH
    )


class Gather:
    def __init__(self, ring, buf, ring_sems, sib_sems):
        self.ring, self.buf = ring, buf
        self.rs, self.ss = ring_sems, sib_sems
        self.half = buf.shape[1] // 2
        self.sub = self.half // SUBS

    def at(self, d, t):
        return self.ring.pos - t if d == 0 else self.ring.pos + t

    def part(self, owner, d, u):
        return self.buf.at[owner, pl.ds(d * self.half + u * self.sub, self.sub)]

    def hop(self, d, u, t):
        ref = self.part(self.ring.owner(self.at(d, t)), d, u)
        return remote(ref, ref, self.rs.at[0, d, u, t], self.rs.at[1, d, u, t], self.ring.next[d])

    def hop_in(self, d, u, t):
        ref = self.part(self.ring.owner(self.at(d, t + 1)), d, u)
        return remote(ref, ref, self.rs.at[0, d, u, t], self.rs.at[1, d, u, t], self.ring.next[d])

    def across(self, d, u, t):
        ref = self.part(self.ring.owner(self.at(d, t)), d, u)
        return remote(ref, ref, self.ss.at[0, d, u, t], self.ss.at[1, d, u, t], self.ring.sibling)

    def across_in(self, d, u, t):
        ref = self.part(self.ring.owner(self.at(d, t), True), d, u)
        return remote(ref, ref, self.ss.at[0, d, u, t], self.ss.at[1, d, u, t], self.ring.sibling)

    def step(self, t, first=False, last=False):
        for u in range(SUBS):
            for d in range(2):
                if not first:
                    self.hop_in(d, u, t - 1).wait_recv()
                if not last:
                    self.hop(d, u, t).start()
                self.across(d, u, t).start()

    def wait_across(self, t):
        for u in range(SUBS):
            for d in range(2):
                self.across_in(d, u, t).wait_recv()

    def mine(self, d, t):
        return self.ring.owner(self.at(d, t))

    def theirs(self, d, t):
        return self.ring.owner(self.at(d, t), True)

    def finish(self):
        @pl.loop(0, self.ring.n)
        def _(t):
            for u in range(SUBS):
                for d in range(2):
                    self.across(d, u, t).wait_send()

        @pl.loop(0, self.ring.n - 1)
        def _(t):
            for u in range(SUBS):
                for d in range(2):
                    self.hop(d, u, t).wait_send()


class Scatter:
    def __init__(self, ring, term, land, sib_in, sib_out, ring_sems, sib_sems):
        self.ring, self.term = ring, term
        self.land, self.sib_in, self.sib_out = land, sib_in, sib_out
        self.rs, self.ss = ring_sems, sib_sems
        self.sub = land.shape[2] // SUBS

    def at(self, d, t):
        return self.ring.pos - 1 - t if d == 0 else self.ring.pos + 1 + t

    def across(self, d, t):
        return remote(
            self.sib_out.at[t, d], self.sib_in.at[t, d], self.ss.at[0, d, t], self.ss.at[1, d, t], self.ring.sibling
        )

    def rows(self, u):
        return pl.ds(u * self.sub, self.sub)

    def hop(self, d, u, t, first=False):
        src = self.sib_in.at[0, d, self.rows(u)] if first else self.land.at[t - 1, d, self.rows(u)]
        dst = self.land.at[t, d, self.rows(u)]
        return remote(src, dst, self.rs.at[0, d, u, t], self.rs.at[1, d, u, t], self.ring.next[d])

    def prepare(self, t):
        for d in range(2):
            self.sib_out[t, d] = self.term(self.ring.owner(self.at(d, t), True), d)
            self.across(d, t).start()
        own = [self.term(self.ring.owner(self.at(d, t)), d) for d in range(2)]
        for d in range(2):
            self.across(d, t).wait_recv()
            self.sib_in[t, d] = self.sib_in[t, d] + own[d]

    def start(self):
        for u in range(SUBS):
            for d in range(2):
                self.hop(d, u, 0, True).start()

    def step(self, t):
        for u in range(SUBS):
            for d in range(2):
                into = self.land.at[t - 1, d, self.rows(u)]
                remote(into, into, self.rs.at[0, d, u, t - 1], self.rs.at[1, d, u, t - 1], self.ring.next[d]).wait_recv()
                self.land[t - 1, d, self.rows(u)] = self.land[t - 1, d, self.rows(u)] + self.sib_in[t, d, self.rows(u)]
                self.hop(d, u, t).start()

    def result(self, d):
        last = self.ring.n - 1
        for u in range(SUBS):
            into = self.land.at[last - 1, d, self.rows(u)]
            remote(
                into, into, self.rs.at[0, d, u, last - 1], self.rs.at[1, d, u, last - 1], self.ring.next[d]
            ).wait_recv()
        return self.land[last - 1, d] + self.sib_in[last, d]

    def finish(self):
        for u in range(SUBS):
            for d in range(2):
                self.hop(d, u, 0, True).wait_send()

        @pl.loop(1, self.ring.n - 1)
        def _(t):
            for u in range(SUBS):
                for d in range(2):
                    self.hop(d, u, t).wait_send()

        @pl.loop(0, self.ring.n)
        def _(t):
            for d in range(2):
                self.across(d, t).wait_send()


def columns(owner, slim):
    return pl.ds(pl.multiple_of(owner * slim, 128), slim)


def sums_kernel(
    n_rows, left_ref, factor_ref, core_ref, coef_ref, dual_ref, tile_ref,
    fac, land, sib_in, sib_out, raw, flat, load, raws, flats, rs, ss,
):
    ring = Ring(n_rows)
    slim = dual_ref.shape[1]
    width = dual_ref.shape[0]
    n = ring.n
    deep = raw.shape[1]

    def piece(offset, slot):
        chip = ring.owner(ring.pos + offset) // 2
        cols = columns(chip, 2 * slim)
        return pltpu.make_async_copy(factor_ref.at[:, cols], fac.at[:, cols], load.at[slot])

    order = [-1, 1] + [o for i in range(2, n // 2) for o in (-i, i)] + [n // 2, 0]
    pieces = [piece(offset, slot) for slot, offset in enumerate(order)]
    for copy in pieces:
        copy.start()

    def fetch(t):
        rows = pl.ds(pl.multiple_of(t * deep, 16), deep)
        return pltpu.make_async_copy(core_ref.at[rows], raw.at[t % 2], raws.at[t % 2])

    def keep(t):
        rows = pl.ds(pl.multiple_of(t * deep, 16), deep)
        return pltpu.make_async_copy(flat.at[t % 2], tile_ref.at[rows], flats.at[t % 2])

    def flatten(t, first=False, last=False):
        fetch(t).wait()
        if not last:
            fetch(t + 1).start()
        if not first:
            keep(t - 1).wait()

        @pl.loop(0, deep // 32)
        def _(i):
            rows = pl.ds(pl.multiple_of(i * 32, 32), 32)
            for k in range(2):
                flat[t % 2, rows, k * slim : (k + 1) * slim] = raw[t % 2, rows, k, :]

        keep(t).start()

    fetch(0).start()
    ring.enter(False)

    def term(owner, d):
        return jnp.dot(
            left_ref[d * width : (d + 1) * width, :], fac[:, columns(owner, slim)], preferred_element_type=F32
        )

    sums = Scatter(ring, term, land, sib_in, sib_out, rs, ss)
    pieces[0].wait()
    pieces[1].wait()
    sums.prepare(0)
    sums.start()
    for copy in pieces[2:]:
        copy.wait()
    sums.prepare(1)
    flatten(0, first=True)

    @pl.loop(1, n - 1)
    def _(t):
        sums.step(t)
        sums.prepare(t + 1)
        flatten(t)

    flatten(n - 1, last=True)
    coef_ref[...] = sums.result(0)
    dual_ref[...] = sums.result(1)
    keep(n - 1).wait()
    sums.finish()


def mix_kernel(
    n_rows, coef_ref, own_ref, core_ref, dual_ref, weight_ref,
    core, buf, acc, swap, coefs, pairs, land, sib_in, sib_out, load, grs, gss, rs, ss, xs,
):
    ring = Ring(n_rows)
    bulk = pltpu.make_async_copy(core_ref, core, load.at[0])
    bulk.start()
    buf[ring.row] = own_ref[...]
    acc[...] = jnp.zeros_like(acc)
    slim = own_ref.shape[1]
    gather = Gather(ring, buf, grs, gss)
    half = gather.half

    def consume(owner, d):
        pair = halves(buf[owner, d * half : (d + 1) * half, :])
        both = jnp.dot(pair, core[columns(owner, slim), :], preferred_element_type=F32)
        both = both[:half] + both[half:]
        for k in range(2):
            acc[k, d * half : (d + 1) * half, :] += both[:, k * slim : (k + 1) * slim]

    def term(owner, d):
        rows = columns(owner, slim)
        both = lax.dot_general(pairs[0, d], core[rows, :slim], NT, preferred_element_type=F32)
        both = both + lax.dot_general(pairs[1, d], core[rows, slim:], NT, preferred_element_type=F32)
        return both[:half] + both[half:]

    ring.enter(True)
    other = remote(coef_ref, coefs, xs.at[0], xs.at[1], ring.partner)
    other.start()
    gather.step(0, first=True)
    for d in range(2):
        pairs[ring.rank, d] = halves(coef_ref[d * half : (d + 1) * half, :])
    bulk.wait()
    for d in range(2):
        consume(gather.mine(d, 0), d)
    other.wait_recv()
    for d in range(2):
        pairs[1 - ring.rank, d] = halves(coefs[d * half : (d + 1) * half, :])
    sums = Scatter(ring, term, land, sib_in, sib_out, rs, ss)
    sums.prepare(0)
    sums.start()
    sums.prepare(1)

    @pl.loop(1, ring.n - 1)
    def _(t):
        gather.step(t)
        gather.wait_across(t - 1)
        for d in range(2):
            consume(gather.theirs(d, t - 1), d)
            consume(gather.mine(d, t), d)
        sums.step(t)
        sums.prepare(t + 1)

    gather.step(ring.n - 1, last=True)
    gather.wait_across(ring.n - 2)
    for d in range(2):
        consume(gather.theirs(d, ring.n - 2), d)
        consume(gather.mine(d, ring.n - 1), d)
    gather.wait_across(ring.n - 1)
    for d in range(2):
        consume(gather.theirs(d, ring.n - 1), d)
    move = remote(acc.at[1 - ring.rank], swap, xs.at[2], xs.at[3], ring.partner)
    move.start()
    for d in range(2):
        weight_ref[d * half : (d + 1) * half, :] = sums.result(d)
    move.wait_recv()
    dual_ref[...] = acc[ring.rank] + swap[...]
    move.wait_send()
    other.wait_send()
    gather.finish()
    sums.finish()


def spread_kernel(
    n_rows, dual_ref, weight_ref, factor_ref, duals_ref, weights_ref, product_ref,
    fac, dbuf, wbuf, load, outs, drs, dss, wrs, wss,
):
    ring = Ring(n_rows)
    bulk = pltpu.make_async_copy(factor_ref, fac, load.at[0])
    bulk.start()
    dbuf[ring.row] = dual_ref[...]
    wbuf[ring.row] = weight_ref[...]
    product_ref[...] = jnp.zeros_like(product_ref)
    slim = dual_ref.shape[1]
    duals = Gather(ring, dbuf, drs, dss)
    weights = Gather(ring, wbuf, wrs, wss)
    half = duals.half

    def out(which, other, d, t):
        buf, ref = ((dbuf, duals_ref), (wbuf, weights_ref))[which]
        owner = duals.theirs(d, t) if other else duals.mine(d, t)
        rows = pl.ds(d * half, half)
        return pltpu.make_async_copy(buf.at[owner, rows], ref.at[owner, rows], outs.at[which, other, d, t])

    def consume(owner, d):
        right = halves(dbuf[owner, d * half : (d + 1) * half, :])
        both = lax.dot_general(fac[:, columns(owner, slim)], right, NT, preferred_element_type=F32)
        product_ref[:, d * half : (d + 1) * half] += both[:, :half] + both[:, half:]

    def use(other, t):
        for d in range(2):
            out(0, other, d, t).start()
            out(1, other, d, t).start()
        for d in range(2):
            consume(duals.theirs(d, t) if other else duals.mine(d, t), d)

    def crossed(t):
        duals.wait_across(t)
        weights.wait_across(t)

    ring.enter(False)
    duals.step(0, first=True)
    weights.step(0, first=True)
    bulk.wait()
    use(0, 0)

    @pl.loop(1, ring.n - 1)
    def _(t):
        duals.step(t)
        crossed(t - 1)
        use(1, t - 1)
        weights.step(t)
        use(0, t)

    duals.step(ring.n - 1, last=True)
    weights.step(ring.n - 1, last=True)
    crossed(ring.n - 2)
    use(1, ring.n - 2)
    use(0, ring.n - 1)
    crossed(ring.n - 1)
    use(1, ring.n - 1)

    @pl.loop(0, ring.n)
    def _(t):
        for which in range(2):
            for other in range(2):
                for d in range(2):
                    out(which, other, d, t).wait()

    duals.finish()
    weights.finish()


def outer_kernel(scale_ref, left_ref, rank_ref, weights_ref, duals_ref, out_ref):
    first = lax.axis_index("rank") * (out_ref.shape[1] * pl.num_programs(0)) + pl.program_id(0) * out_ref.shape[1]
    right = halves(jnp.concatenate([weights_ref[0], duals_ref[0]], axis=0))
    scale = scale_ref[0]
    rows = left_ref.shape[0]
    tile = min(rows, 256)
    for r in range(0, rows, tile):
        total = jnp.dot(left_ref[r : r + tile, :], right, preferred_element_type=F32)
        where = first + lax.broadcasted_iota(jnp.int32, total.shape, 1)
        keep = where <= rank_ref[r : r + tile, :]
        out_ref[r : r + tile, :] = jnp.where(keep, total * scale, 0.0).astype(BF16)


def sems(*shape):
    return pltpu.SemaphoreType.DMA(shape)


def params(n):
    return pltpu.CompilerParams(collective_id=n, has_side_effects=True, vmem_limit_bytes=60 * 2**20)


def shape_of(*shape):
    return jax.ShapeDtypeStruct(shape, F32)


def ranks_of_rows(pivots, first_row, rows_dev):
    total = pivots.shape[0]
    local = pivots - first_row
    number = jnp.arange(1, total + 1, dtype=jnp.int32)
    high = (local >> 7)[None, :] == jnp.arange(rows_dev // 128, dtype=jnp.int32)[:, None]
    low = ((local & 127)[:, None] == jnp.arange(128, dtype=jnp.int32)[None, :]).astype(BF16)
    upper = jnp.where(high, number >> 7, 0).astype(BF16)
    lower = jnp.where(high, number & 127, 0).astype(BF16)
    found = jnp.dot(jnp.concatenate([upper, lower], axis=0), low, preferred_element_type=F32)
    found = found.astype(jnp.int32).reshape(2, rows_dev)
    found = found[0] * 128 + found[1]
    return jnp.where(found > 0, found - 1, total)


def ring_body(factor, probes, cotangent, core_inverse, pivots, noise):
    rows_dev, block_cols = factor.shape
    width = probes.shape[1]
    n_rows = lax.axis_size("rows")
    slim = block_cols // n_rows
    n = n_rows // 2
    half = width // 2
    scale = noise[0]
    left = jnp.concatenate([probes.T, cotangent.T], axis=0)
    deep = block_cols // n
    ring_sem = sems(2, 2, SUBS, n)
    sib_sem = sems(2, 2, n)
    bucket = pltpu.VMEM((n_rows, width, slim), F32)
    block = pltpu.VMEM((width, slim), F32)
    coef_own, dual_in, core_tile = pl.pallas_call(
        functools.partial(sums_kernel, n_rows),
        out_shape=(
            shape_of(width, slim),
            shape_of(width, slim),
            jax.ShapeDtypeStruct((block_cols, 2 * slim), BF16),
        ),
        in_specs=[VMEM, ANY, ANY],
        out_specs=(VMEM, VMEM, ANY),
        scratch_shapes=[
            pltpu.VMEM(factor.shape, BF16),
            pltpu.VMEM((n - 1, 2, width, slim), F32),
            pltpu.VMEM((n, 2, width, slim), F32),
            pltpu.VMEM((n, 2, width, slim), F32),
            pltpu.VMEM((2, deep, 2, slim), BF16),
            pltpu.VMEM((2, deep, 2 * slim), BF16),
            sems(n), sems(2), sems(2), ring_sem, sib_sem,
        ],
        compiler_params=params(0),
        name="sums",
    )(left, factor, core_inverse)
    dual_own, weight_own = pl.pallas_call(
        functools.partial(mix_kernel, n_rows),
        out_shape=(shape_of(width, slim), shape_of(width, slim)),
        in_specs=[VMEM, VMEM, ANY],
        out_specs=(VMEM, VMEM),
        scratch_shapes=[
            pltpu.VMEM(core_tile.shape, BF16),
            bucket,
            pltpu.VMEM((2, width, slim), F32),
            block,
            block,
            pltpu.VMEM((2, 2, width, slim), BF16),
            pltpu.VMEM((n - 1, 2, half, slim), F32),
            pltpu.VMEM((n, 2, half, slim), F32),
            pltpu.VMEM((n, 2, half, slim), F32),
            sems(1), ring_sem, ring_sem, ring_sem, sib_sem, sems(4),
        ],
        compiler_params=params(1),
        name="mix",
    )(coef_own, dual_in, core_tile)
    duals, weights, product = pl.pallas_call(
        functools.partial(spread_kernel, n_rows),
        out_shape=(shape_of(n_rows, width, slim), shape_of(n_rows, width, slim), shape_of(rows_dev, width)),
        in_specs=[VMEM, VMEM, ANY],
        out_specs=(ANY, ANY, VMEM),
        scratch_shapes=[
            pltpu.VMEM(factor.shape, BF16),
            bucket,
            bucket,
            sems(1), sems(2, 2, 2, n), ring_sem, ring_sem, ring_sem, ring_sem,
        ],
        compiler_params=params(2),
        name="spread",
    )(dual_own, weight_own, factor)
    product = product + lax.ppermute(product, "rank", [(0, 1), (1, 0)])
    probe_grad = ((cotangent.astype(F32) - product) / scale).astype(BF16)
    pivot_rank = ranks_of_rows(pivots, lax.axis_index("rows") * rows_dev, rows_dev)
    pair = jnp.concatenate([cotangent, probes, cotangent, probes], axis=1)
    block = pl.BlockSpec((1, width, slim), lambda j: (j, 0, 0))
    grads = pl.pallas_call(
        outer_kernel,
        grid=(n_rows,),
        out_shape=jax.ShapeDtypeStruct(factor.shape, BF16),
        in_specs=[
            pl.BlockSpec(memory_space=pltpu.SMEM),
            pl.BlockSpec((rows_dev, 4 * width), lambda j: (0, 0)),
            pl.BlockSpec((rows_dev, 1), lambda j: (0, 0)),
            block,
            block,
        ],
        out_specs=pl.BlockSpec((rows_dev, slim), lambda j: (0, j)),
        compiler_params=pltpu.CompilerParams(vmem_limit_bytes=60 * 2**20),
        cost_estimate=pl.CostEstimate(
            flops=8 * rows_dev * width * block_cols,
            bytes_accessed=2 * rows_dev * block_cols + 8 * width * block_cols,
            transcendentals=0,
        ),
        name="outer",
    )(-1.0 / noise, pair, pivot_rank[:, None], weights, duals)
    return probe_grad, grads


def body(factor, probes, cotangent, core_inverse, pivots, noise):
    highest = lax.Precision.HIGHEST
    rows_dev = factor.shape[0]
    block_cols = factor.shape[1]
    width = probes.shape[1]
    n_rows = lax.axis_size("rows")
    n_rank = lax.axis_size("rank")
    slim = block_cols // n_rows
    row_index = lax.axis_index("rows")
    rank_index = lax.axis_index("rank")
    scale = noise[0]
    core_tile = core_inverse.reshape(block_cols, n_rank * slim).astype(jnp.float32)
    contract = (((0,), (0,)), ((), ()))
    stacked = jnp.concatenate([probes, cotangent], axis=1)
    partial_sums = lax.dot_general(factor, stacked, contract, preferred_element_type=jnp.float32)
    share = lax.psum_scatter(partial_sums, "rows", scatter_dimension=0, tiled=True)
    coef_part = share[:, :width]
    dual_full = lax.all_gather(share[:, width:], "rows", axis=0, tiled=True)
    coef_cols = lax.all_gather(coef_part, "rank", axis=0, tiled=True)
    weights_blk = lax.psum(
        jnp.dot(core_tile, coef_cols, precision=highest, preferred_element_type=jnp.float32), "rows"
    )
    dual_part = lax.psum_scatter(
        lax.dot_general(
            core_tile, dual_full, contract, precision=highest, preferred_element_type=jnp.float32
        ),
        "rank",
        scatter_dimension=0,
        tiled=True,
    )
    duals_blk = lax.all_gather(dual_part, "rows", axis=0, tiled=True)
    local_product = jnp.dot(
        factor.astype(jnp.float32), duals_blk, precision=highest, preferred_element_type=jnp.float32
    )
    correction = lax.psum(local_product, "rank")
    probe_grad = ((cotangent.astype(jnp.float32) - correction) / scale).astype(jnp.bfloat16)
    left_side = jnp.concatenate([cotangent, probes], axis=1).astype(jnp.float32)
    right_side = jnp.concatenate([weights_blk, duals_blk], axis=1)
    outer_sum = lax.dot_general(
        left_side,
        right_side,
        (((1,), (1,)), ((), ())),
        precision=highest,
        preferred_element_type=jnp.float32,
    )
    grads = -outer_sum / scale
    local_rows = pivots - row_index * rows_dev
    inside = (local_rows >= 0) & (local_rows < rows_dev)
    target = jnp.where(inside, local_rows, rows_dev)
    total_rank = pivots.shape[0]
    pivot_rank = (
        jnp.full((rows_dev + 1,), total_rank, jnp.int32)
        .at[target]
        .set(jnp.arange(total_rank, dtype=jnp.int32))[:rows_dev]
    )
    columns = rank_index * block_cols + jnp.arange(block_cols, dtype=jnp.int32)
    grads = jnp.where(columns[None, :] > pivot_rank[:, None], jnp.float32(0.0), grads)
    return (probe_grad, grads.astype(jnp.bfloat16))


def solution(mesh):
    placed = (
        P("rows", "rank"),
        P("rows", None),
        P("rows", None),
        P("rank", None, "rows"),
        P(),
        P(),
    )
    n_rows, n_rank = mesh.shape["rows"], mesh.shape["rank"]

    def chosen(factor, probes, cotangent, core_inverse, pivots, noise):
        slim = factor.shape[1] // n_rows
        fits = n_rank == 2 and n_rows % 4 == 0 and n_rows >= 8 and slim % 128 == 0 and factor.shape[0] % 128 == 0
        run = ring_body if fits and pivots.shape[0] <= 2**15 else body
        return run(factor, probes, cotangent, core_inverse, pivots, noise)

    return jax.shard_map(
        chosen,
        mesh=mesh,
        in_specs=placed,
        out_specs=(P("rows", None), P("rows", "rank")),
        check_vma=False,
    )
```
